32 devices in a mesh: row: 8 (over y, x, core), col: 4 (over z).
Axes of the slice: x: 2, y: 2, z: 4, core: 2. Of those that a mesh axis runs over, the one named last changes fastest.
Arguments:
- eigvecs: float32 [2048, 8192], P(('row', 'col')), may hold values from -6 to 6
- reflectors: float32 [1024, 8192], P('col', 'row'), may hold values from -0.0625 to 0.0625
Outputs:
- transformed: float32 [2048, 8192], P(('row', 'col'))
The draws below stay inside these ranges and needn't reach their ends.
All inputs are finite; a program needn't handle non-finite values.
Results may differ from the reference program's by a relative error of at most 0.00015.
Values sent between devices are 32-bit elements; how exact they have to be, the bound alone decides.
No kernel may reach another device: no remote copies, remote signals or barrier semaphores. Data moves between devices by JAX's collectives and lax.ppermute only.
A program may use at most 64 MiB of HBM per device.

```python
import jax
import jax.numpy as jnp
from jax import lax

K = 2048
B = 256
PANELS = 4
N = 8192


def steps_of(rng, shape, cuts, low, high):
    loudness, own = 1.0, jax.random.fold_in(rng, 6)
    for axis_at, blocks in cuts:
        heights = jnp.exp(jax.random.uniform(jax.random.fold_in(own, axis_at), (blocks,), jnp.float32, low / len(cuts), high / len(cuts)))
        loudness = loudness * jnp.repeat(heights, shape[axis_at] // blocks).reshape([-1 if axis == axis_at else 1 for axis in range(len(shape))])
    return loudness


def normal_values(own_key, shape, width, bound, shards=(), held_as=jnp.bfloat16):
    entries = width * jax.random.normal(own_key, shape, jnp.float32)
    if shards:
        entries = entries * steps_of(own_key, shape, shards, -0.22, 0.18)
    return jnp.clip(entries, -bound, bound).astype(held_as)


def setup_inputs(seed: int = 0) -> dict:
    streams_of = jax.random.split(jax.random.key(seed), 3)
    eigvecs = normal_values(streams_of[0], (K, N), 1.0, 6.0, ((0, 32),), jnp.float32)
    reflectors = normal_values(streams_of[1], (PANELS * B, N), N ** -0.5, 0.0625, ((0, 4), (1, 8)), jnp.float32)
    return {"eigvecs": eigvecs, "reflectors": reflectors}


def masked_vectors(block, which):
    rows_all = lax.broadcasted_iota(jnp.int32, block.shape, 1)
    starts = lax.broadcasted_iota(jnp.int32, block.shape, 0) + which * B
    unit = jnp.where(rows_all == starts, jnp.ones_like(block), jnp.zeros_like(block))
    return jnp.where(rows_all > starts, block, unit)

def upper_factor(gram):
    return jnp.triu(gram, 1) + jnp.diag(jnp.diag(gram) * 0.5)

def reference(eigvecs, reflectors):
    current = eigvecs
    for which in reversed(range(PANELS)):
        vectors = masked_vectors(reflectors[which * B:(which + 1) * B, :], which)
        gram = jnp.dot(vectors.astype(jnp.float32), vectors.T.astype(jnp.float32), precision=lax.Precision.HIGHEST, preferred_element_type=jnp.float32)
        factor = upper_factor(gram)
        product = jnp.dot(current.astype(jnp.float32), vectors.T.astype(jnp.float32), precision=lax.Precision.HIGHEST, preferred_element_type=jnp.float32)
        solved = lax.linalg.triangular_solve(factor, product, left_side=False, lower=False, transpose_a=True)
        current = current - jnp.dot(solved.astype(jnp.float32), vectors.astype(jnp.float32), precision=lax.Precision.HIGHEST, preferred_element_type=jnp.float32)
    return current
```

```python
import jax
import jax.numpy as jnp
from jax import lax
from jax.experimental import pallas as pl
from jax.experimental.pallas import tpu as pltpu
from jax.sharding import PartitionSpec as P

B = 256
PANELS = 4


def masked_vectors(block, which, row_base):
    rows_all = lax.broadcasted_iota(jnp.int32, block.shape, 1) + row_base
    starts = lax.broadcasted_iota(jnp.int32, block.shape, 0) + which * B
    unit = jnp.where(rows_all == starts, jnp.ones_like(block), jnp.zeros_like(block))
    return jnp.where(rows_all > starts, block, unit)


def upper_factor(gram):
    return jnp.triu(gram, 1) + jnp.diag(jnp.diag(gram) * 0.5)


def hdot(left, right):
    return jnp.dot(left, right, precision=lax.Precision.HIGHEST, preferred_element_type=jnp.float32)


def apply_inverse(product, factor):
    order = factor.shape[0]
    diagonal = jnp.diagonal(factor)
    nilpotent = -jnp.triu(factor, 1) / diagonal[:, None]
    solved = product / diagonal[None, :]
    power = nilpotent
    solved = solved + hdot(solved, power.T)
    for level in range((order - 1).bit_length() - 1):
        power = hdot(power, power)
        solved = solved + hdot(solved, power.T)
    return solved


def general(eigvecs, reflectors):
    current = lax.all_to_all(eigvecs, "row", split_axis=1, concat_axis=0, tiled=True)
    gathered = lax.all_gather(reflectors, "col", axis=0, tiled=True)
    local_rows = current.shape[1]
    row_base = lax.axis_index("row") * local_rows
    blocks = []
    for which in range(PANELS):
        blocks.append(masked_vectors(gathered[which * B : (which + 1) * B, :], which, row_base))
    gram_local = jnp.stack([hdot(vectors, vectors.T) for vectors in blocks])
    gram_all = lax.psum(gram_local, "row")
    for which in reversed(range(PANELS)):
        vectors = blocks[which]
        factor = upper_factor(gram_all[which])
        partial_value = hdot(current, vectors.T)
        summed = lax.psum(partial_value, "row")
        solved = apply_inverse(summed, factor)
        current = current - hdot(solved, vectors)
    return lax.all_to_all(current, "row", split_axis=0, concat_axis=1, tiled=True)


def nt(left, right):
    return lax.dot_general(
        left, right, (((1,), (1,)), ((), ())), precision=lax.Precision.HIGH, preferred_element_type=jnp.float32
    )


def nn(left, right):
    return lax.dot_general(
        left, right, (((1,), (0,)), ((), ())), precision=lax.Precision.HIGH, preferred_element_type=jnp.float32
    )


def kdot(left, right, contract=0):
    return lax.dot_general(
        left,
        right,
        (((1,), (contract,)), ((), ())),
        precision=lax.Precision.HIGHEST,
        preferred_element_type=jnp.float32,
    )


def inverse_kernel(gram_ref, out_ref):
    gram = gram_ref[...]
    rows = lax.broadcasted_iota(jnp.int32, gram.shape, 0)
    cols = lax.broadcasted_iota(jnp.int32, gram.shape, 1)
    inv = jnp.where(rows == cols, 2.0 / gram, 0.0)
    size = 1
    while size < gram.shape[0]:
        pick = (rows // (2 * size) == cols // (2 * size)) & (rows % (2 * size) >= size) & (cols % (2 * size) < size)
        inv = inv - kdot(kdot(inv, jnp.where(pick, gram, 0.0)), inv)
        size *= 2
    out_ref[...] = inv


def inverse(gram):
    return pl.pallas_call(inverse_kernel, out_shape=jax.ShapeDtypeStruct(gram.shape, jnp.float32))(gram)


def solve_kernel(where_ref, p_ref, g_ref, t_ref, s_ref):
    c = where_ref[0]
    for which in reversed(range(PANELS)):
        slot = c ^ which
        value = p_ref[slot]
        for later in range(which + 1, PANELS):
            other = c ^ later
            solved = s_ref[other]

            def direct(solved=solved, other=other):
                return kdot(solved, g_ref[other * (other - 1) // 2 + slot], 0)

            def flipped(solved=solved, other=other):
                return kdot(solved, g_ref[slot * (slot - 1) // 2 + other], 1)

            value = value - lax.cond(other > slot, direct, flipped)
        s_ref[slot] = kdot(value, t_ref[which])


def solve(c, products, grams, inverses):
    return pl.pallas_call(
        solve_kernel,
        out_shape=jax.ShapeDtypeStruct(products.shape, jnp.float32),
        in_specs=[pl.BlockSpec(memory_space=pltpu.SMEM)] + [pl.BlockSpec(memory_space=pltpu.VMEM)] * 3,
        out_specs=pl.BlockSpec(memory_space=pltpu.VMEM),
        compiler_params=pltpu.CompilerParams(vmem_limit_bytes=24 * 2**20),
    )(c.reshape(1).astype(jnp.int32), products, grams, inverses)


def panels_on_cols(eigvecs, reflectors, chips):
    width = reflectors.shape[1]
    r, c = lax.axis_index("row"), lax.axis_index("col")
    core, chip = r % 2, r // 2
    mine = eigvecs.shape[0]

    def across(value, x):
        return lax.ppermute(value, "row", [(i, i ^ (2 * x)) for i in range(2 * chips)])

    def sibling(value):
        return lax.ppermute(value, "row", [(i, i ^ 1) for i in range(2 * chips)])

    def zmove(value, pairs):
        return lax.ppermute(value, "col", pairs)

    def by_chip(value):
        bit = 1
        while bit < chips:
            turned = value[jnp.array([i ^ bit for i in range(chips)])] if False else jnp.stack(
                [value[i ^ bit] for i in range(chips)]
            )
            value = jnp.where((chip & bit) != 0, turned, value)
            bit *= 2
        return value

    def total(products, grams):
        n_p, n_g = len(products), len(grams)
        part = B // 2 // chips
        packed = [p.reshape(chips, mine, B) for p in products]
        packed += [by_chip(g.reshape(chips, part, B)) for g in grams]
        packed = jnp.concatenate(packed, axis=1)
        held = packed[0]
        for x in range(1, chips):
            held = held + across(packed[x], x)
        full = jnp.stack([held] + [across(held, x) for x in range(1, chips)])
        out_p = [full[:, i * mine : (i + 1) * mine].reshape(chips * mine, B) for i in range(n_p)]
        out_g = None
        if n_g:
            halves = full[:, n_p * mine :].reshape(chips, n_g, part, B)
            halves = by_chip(halves).transpose(1, 0, 2, 3).reshape(n_g, B // 2, B)
            others = sibling(halves)
            first, second = jnp.where(core == 0, halves, others), jnp.where(core == 0, others, halves)
            out_g = jnp.concatenate([first, second], axis=1)
        return out_p, out_g

    vectors = masked_vectors(reflectors, c, r * width)
    near = zmove(vectors, [(0, 1), (1, 0), (2, 3), (3, 2)])
    inner = zmove(vectors, [(1, 2), (2, 1)])

    def piece(x):
        start = (chip ^ x) * 2 * width
        return jnp.stack(
            [
                lax.dynamic_slice(eigvecs, (0, start + core * width), (mine, width)),
                lax.dynamic_slice(eigvecs, (0, start + (1 - core) * width), (mine, width)),
            ]
        )

    pieces = [piece(0)] + [across(piece(x), x) for x in range(1, chips)]
    e_m = jnp.concatenate([p[0] for p in pieces])
    e_o = jnp.concatenate([p[1] for p in pieces])

    edge = (c == 0) | (c == 3)
    second_out = zmove(inner, [(1, 0), (2, 3)])
    second_in = zmove(near, [(1, 2), (2, 1)])
    second = jnp.where(edge, second_out, second_in)
    third_out = zmove(second_in, [(1, 0), (2, 3)])
    third = jnp.where(edge, third_out, inner)

    slots = []
    for v in (vectors, near, second, third):
        slots.append((v, sibling(v)))

    def product(slot):
        m, o = slots[slot]
        return nt(e_m, m) + nt(e_o, o)

    def gram(slot, other):
        m, o = slots[slot]
        hm = lax.dynamic_slice(m, (core * (B // 2), 0), (B // 2, width))
        ho = lax.dynamic_slice(o, (core * (B // 2), 0), (B // 2, width))
        return nt(hm, slots[other][0]) + nt(ho, slots[other][1])

    p_01, g_01 = total([product(0), product(1)], [gram(0, 0), gram(1, 0)])
    inv = inverse(g_01[0])
    share = B // (2 * chips)
    inv_part = lax.dynamic_slice(inv, (r * share, 0), (share, B))
    inverses = lax.all_gather(inv_part, ("col", "row"), axis=0, tiled=True).reshape(PANELS, B, B)
    p_2, g_2 = total([product(2)], [gram(2, 0), gram(2, 1)])
    p_3, g_3 = total([product(3)], [gram(3, 0), gram(3, 1), gram(3, 2)])
    products = jnp.stack(p_01 + p_2 + p_3)
    grams = jnp.concatenate([g_01[1:], g_2, g_3])
    solved = solve(c, products, grams, inverses)
    s_all = jnp.concatenate([solved[i] for i in range(PANELS)], axis=1)
    v_m = jnp.concatenate([m for m, _ in slots])
    v_o = jnp.concatenate([o for _, o in slots])
    done_m = e_m - nn(s_all, v_m)
    done_o = e_o - nn(s_all, v_o)
    result = jnp.zeros_like(eigvecs)
    for x in range(chips):
        rows = slice(x * mine, (x + 1) * mine)
        both = jnp.stack([done_m[rows], done_o[rows]])
        if x:
            both = across(both, x)
        start = (chip ^ x) * 2 * width
        result = lax.dynamic_update_slice(result, both[0], (0, start + core * width))
        result = lax.dynamic_update_slice(result, both[1], (0, start + (1 - core) * width))
    return result


def solution(mesh):
    rows, cols = mesh.shape["row"], mesh.shape["col"]
    placed = (P(("row", "col"), None), P("col", "row"))

    def shards(eigvecs, reflectors):
        if cols == PANELS and reflectors.shape[0] == B and rows >= 4 and rows & (rows - 1) == 0 and B % (16 * rows) == 0:
            return panels_on_cols(eigvecs, reflectors, rows // 2)
        return general(eigvecs, reflectors)

    return jax.shard_map(shards, mesh=mesh, in_specs=placed, out_specs=P(("row", "col"), None), check_vma=False)
```

```python
import jax
import jax.numpy as jnp
from jax import lax
from jax.experimental import pallas as pl
from jax.experimental.pallas import tpu as pltpu
from jax.sharding import PartitionSpec as P

B = 256
PANELS = 4


def masked_vectors(block, which, row_base):
    rows_all = lax.broadcasted_iota(jnp.int32, block.shape, 1) + row_base
    starts = lax.broadcasted_iota(jnp.int32, block.shape, 0) + which * B
    unit = jnp.where(rows_all == starts, jnp.ones_like(block), jnp.zeros_like(block))
    return jnp.where(rows_all > starts, block, unit)


def upper_factor(gram):
    return jnp.triu(gram, 1) + jnp.diag(jnp.diag(gram) * 0.5)


def hdot(left, right):
    return jnp.dot(left, right, precision=lax.Precision.HIGHEST, preferred_element_type=jnp.float32)


def apply_inverse(product, factor):
    order = factor.shape[0]
    diagonal = jnp.diagonal(factor)
    nilpotent = -jnp.triu(factor, 1) / diagonal[:, None]
    solved = product / diagonal[None, :]
    power = nilpotent
    solved = solved + hdot(solved, power.T)
    for level in range((order - 1).bit_length() - 1):
        power = hdot(power, power)
        solved = solved + hdot(solved, power.T)
    return solved


def general(eigvecs, reflectors):
    current = lax.all_to_all(eigvecs, "row", split_axis=1, concat_axis=0, tiled=True)
    gathered = lax.all_gather(reflectors, "col", axis=0, tiled=True)
    local_rows = current.shape[1]
    row_base = lax.axis_index("row") * local_rows
    blocks = []
    for which in range(PANELS):
        blocks.append(masked_vectors(gathered[which * B : (which + 1) * B, :], which, row_base))
    gram_local = jnp.stack([hdot(vectors, vectors.T) for vectors in blocks])
    gram_all = lax.psum(gram_local, "row")
    for which in reversed(range(PANELS)):
        vectors = blocks[which]
        factor = upper_factor(gram_all[which])
        partial_value = hdot(current, vectors.T)
        summed = lax.psum(partial_value, "row")
        solved = apply_inverse(summed, factor)
        current = current - hdot(solved, vectors)
    return lax.all_to_all(current, "row", split_axis=0, concat_axis=1, tiled=True)


def nt(left, right):
    return lax.dot_general(
        left, right, (((1,), (1,)), ((), ())), precision=lax.Precision.HIGH, preferred_element_type=jnp.float32
    )


def nn(left, right):
    return lax.dot_general(
        left, right, (((1,), (0,)), ((), ())), precision=lax.Precision.HIGH, preferred_element_type=jnp.float32
    )


def kdot(left, right, contract=0):
    return lax.dot_general(
        left,
        right,
        (((1,), (contract,)), ((), ())),
        precision=lax.Precision.HIGHEST,
        preferred_element_type=jnp.float32,
    )


def inverse_kernel(gram_ref, out_ref):
    half = gram_ref.shape[0] // 2
    rows = lax.broadcasted_iota(jnp.int32, (half, half), 0)
    cols = lax.broadcasted_iota(jnp.int32, (half, half), 1)
    grams = [gram_ref[:half, :half], gram_ref[half:, half:]]
    inv = [jnp.where(rows == cols, 2.0 / gram, 0.0) for gram in grams]
    size = 1
    while size < half:
        pick = (rows // (2 * size) == cols // (2 * size)) & (rows % (2 * size) >= size) & (cols % (2 * size) < size)
        inner = [kdot(i, jnp.where(pick, gram, 0.0)) for i, gram in zip(inv, grams)]
        inv = [i - kdot(t, i) for i, t in zip(inv, inner)]
        size *= 2
    out_ref[:half, :half] = inv[0]
    out_ref[:half, half:] = jnp.zeros((half, half), jnp.float32)
    out_ref[half:, :half] = -kdot(kdot(inv[1], gram_ref[half:, :half]), inv[0])
    out_ref[half:, half:] = inv[1]


def inverse(gram):
    return pl.pallas_call(inverse_kernel, out_shape=jax.ShapeDtypeStruct(gram.shape, jnp.float32))(gram)


def solve_kernel(where_ref, p_ref, g_ref, t_ref, s_ref):
    c = where_ref[0]
    for which in reversed(range(PANELS)):
        slot = c ^ which
        value = p_ref[slot]
        for later in range(which + 1, PANELS):
            other = c ^ later
            solved = s_ref[other]

            def direct(solved=solved, other=other):
                return kdot(solved, g_ref[other * (other - 1) // 2 + slot], 0)

            def flipped(solved=solved, other=other):
                return kdot(solved, g_ref[slot * (slot - 1) // 2 + other], 1)

            value = value - lax.cond(other > slot, direct, flipped)
        s_ref[slot] = kdot(value, t_ref[which])


def solve(c, products, grams, inverses):
    return pl.pallas_call(
        solve_kernel,
        out_shape=jax.ShapeDtypeStruct(products.shape, jnp.float32),
        in_specs=[pl.BlockSpec(memory_space=pltpu.SMEM)] + [pl.BlockSpec(memory_space=pltpu.VMEM)] * 3,
        out_specs=pl.BlockSpec(memory_space=pltpu.VMEM),
        compiler_params=pltpu.CompilerParams(vmem_limit_bytes=24 * 2**20),
    )(c.reshape(1).astype(jnp.int32), products, grams, inverses)


def panels_on_cols(eigvecs, reflectors, chips):
    width = reflectors.shape[1]
    r, c = lax.axis_index("row"), lax.axis_index("col")
    core, chip = r % 2, r // 2
    mine = eigvecs.shape[0]
    part = B // 2 // chips
    groups = [[2 * i + k for i in range(chips)] for k in range(2)]

    def exchange(value):
        return lax.all_to_all(value, "row", split_axis=0, concat_axis=0, tiled=True, axis_index_groups=groups)

    def across(value, x):
        return lax.ppermute(value, "row", [(i, i ^ (2 * x)) for i in range(2 * chips)])

    def sibling(value):
        return lax.ppermute(value, "row", [(i, i ^ 1) for i in range(2 * chips)])

    def zmove(value, pairs):
        return lax.ppermute(value, "col", pairs)

    def paired(value, axis):
        other = sibling(value)
        return jnp.where(
            core == 0, jnp.concatenate([value, other], axis=axis), jnp.concatenate([other, value], axis=axis)
        )

    def by_chip(value):
        bit = 1
        while bit < chips:
            turned = jnp.stack([value[i ^ bit] for i in range(chips)])
            value = jnp.where((chip & bit) != 0, turned, value)
            bit *= 2
        return value

    def pack(products, grams):
        packed = [p.reshape(chips, mine, B) for p in products]
        packed += [by_chip(g.reshape(chips, part, B)) for g in grams]
        return jnp.concatenate(packed, axis=1)

    def scatter(packed):
        held = packed[0]
        for x in range(1, chips):
            held = held + across(packed[x], x)
        return held

    def collect(held):
        return jnp.stack([held] + [across(held, x) for x in range(1, chips)])

    def unpack(full, n_p, n_g):
        out_p = [full[:, i * mine : (i + 1) * mine].reshape(chips * mine, B) for i in range(n_p)]
        halves = by_chip(full[:, n_p * mine :]).reshape(chips, n_g, part, B).transpose(1, 0, 2, 3)
        return out_p, paired(halves.reshape(n_g, B // 2, B), 1)

    vectors = masked_vectors(reflectors, c, r * width)
    near = zmove(vectors, [(0, 1), (1, 0), (2, 3), (3, 2)])
    inner = zmove(vectors, [(1, 2), (2, 1)])
    slots = [paired(vectors, 1)]

    def product(slot):
        return nt(grid, slots[slot])

    def gram(slot, other):
        half = lax.dynamic_slice(slots[slot], (core * (B // 2), 0), (B // 2, 2 * width))
        return nt(half, slots[other])

    own = gram(0, 0)
    own, eigvecs = lax.optimization_barrier((own, eigvecs))
    g_own = own
    for x in range(1, chips):
        g_own = g_own + across(own, x)
    g_own = paired(g_own, 0)
    pieces = [lax.dynamic_slice(eigvecs, (0, (chip ^ x) * 2 * width), (mine, 2 * width)) for x in range(chips)]
    pieces = pieces[:1] + [across(pieces[x], x) for x in range(1, chips)]
    grid = jnp.concatenate(pieces)

    edge = (c == 0) | (c == 3)
    g_own, near, inner = lax.optimization_barrier((g_own, near, inner))
    second_out = zmove(inner, [(1, 0), (2, 3)])
    second_in = zmove(near, [(1, 2), (2, 1)])
    inv = inverse(g_own)
    inv_part = lax.dynamic_slice(inv, (core * (B // 2) + chip * part, 0), (part, B))
    grid, inv_part = lax.optimization_barrier((grid, inv_part))
    parts = lax.all_to_all(
        jnp.broadcast_to(inv_part, (PANELS, part, B)), "col", split_axis=0, concat_axis=0, tiled=True
    ).reshape(PANELS * part, B)

    slots.append(paired(near, 1))
    packed_01 = pack([product(0), product(1)], [gram(1, 0)])
    second_out, second_in, packed_01 = lax.optimization_barrier((second_out, second_in, packed_01))
    third_out = zmove(second_in, [(1, 0), (2, 3)])
    full_01 = collect(jnp.concatenate([scatter(packed_01), parts]))

    slots.append(paired(jnp.where(edge, second_out, second_in), 1))
    held_2 = scatter(pack([product(2)], [gram(2, 0), gram(2, 1)]))
    third_out, full_01, held_2 = lax.optimization_barrier((third_out, full_01, held_2))
    full_2 = collect(held_2)

    slots.append(paired(jnp.where(edge, third_out, inner), 1))
    held_3 = scatter(pack([product(3)], [gram(3, 0), gram(3, 1), gram(3, 2)]))
    full_2, held_3 = lax.optimization_barrier((full_2, held_3))
    p_01, g_01 = unpack(full_01, 2, 1 + PANELS)
    p_2, g_2 = unpack(full_2, 1, 2)
    p_3, g_3 = unpack(collect(held_3), 1, 3)
    g_01, inverses = g_01[:1], g_01[1:]
    products = jnp.stack(p_01 + p_2 + p_3)
    grams = jnp.concatenate([g_01, g_2, g_3])
    solved = solve(c, products, grams, inverses)
    s_all = jnp.concatenate([solved[i] for i in range(PANELS)], axis=1)
    done = grid - nn(s_all, jnp.concatenate(slots))
    done = done.reshape(chips, mine, 2 * width)
    result = jnp.zeros_like(eigvecs)
    for x in range(chips):
        piece = across(done[x], x) if x else done[x]
        result = lax.dynamic_update_slice(result, piece, (0, (chip ^ x) * 2 * width))
    return result


def solution(mesh):
    rows, cols = mesh.shape["row"], mesh.shape["col"]
    placed = (P(("row", "col"), None), P("col", "row"))

    def shards(eigvecs, reflectors):
        if cols == PANELS and reflectors.shape[0] == B and rows >= 4 and rows & (rows - 1) == 0 and B % (16 * rows) == 0:
            return panels_on_cols(eigvecs, reflectors, rows // 2)
        return general(eigvecs, reflectors)

    return jax.shard_map(shards, mesh=mesh, in_specs=placed, out_specs=P(("row", "col"), None), check_vma=False)
```

```python
import functools

import jax
import jax.numpy as jnp
from jax import lax
from jax.experimental import pallas as pl
from jax.experimental.pallas import tpu as pltpu
from jax.sharding import PartitionSpec as P

B = 256
PANELS = 4


def masked_vectors(block, which, row_base):
    rows_all = lax.broadcasted_iota(jnp.int32, block.shape, 1) + row_base
    starts = lax.broadcasted_iota(jnp.int32, block.shape, 0) + which * B
    unit = jnp.where(rows_all == starts, jnp.ones_like(block), jnp.zeros_like(block))
    return jnp.where(rows_all > starts, block, unit)


def upper_factor(gram):
    return jnp.triu(gram, 1) + jnp.diag(jnp.diag(gram) * 0.5)


def hdot(left, right):
    return jnp.dot(left, right, precision=lax.Precision.HIGHEST, preferred_element_type=jnp.float32)


def apply_inverse(product, factor):
    order = factor.shape[0]
    diagonal = jnp.diagonal(factor)
    nilpotent = -jnp.triu(factor, 1) / diagonal[:, None]
    solved = product / diagonal[None, :]
    power = nilpotent
    solved = solved + hdot(solved, power.T)
    for level in range((order - 1).bit_length() - 1):
        power = hdot(power, power)
        solved = solved + hdot(solved, power.T)
    return solved


def general(eigvecs, reflectors):
    current = lax.all_to_all(eigvecs, "row", split_axis=1, concat_axis=0, tiled=True)
    gathered = lax.all_gather(reflectors, "col", axis=0, tiled=True)
    local_rows = current.shape[1]
    row_base = lax.axis_index("row") * local_rows
    blocks = []
    for which in range(PANELS):
        blocks.append(masked_vectors(gathered[which * B : (which + 1) * B, :], which, row_base))
    gram_local = jnp.stack([hdot(vectors, vectors.T) for vectors in blocks])
    gram_all = lax.psum(gram_local, "row")
    for which in reversed(range(PANELS)):
        vectors = blocks[which]
        factor = upper_factor(gram_all[which])
        partial_value = hdot(current, vectors.T)
        summed = lax.psum(partial_value, "row")
        solved = apply_inverse(summed, factor)
        current = current - hdot(solved, vectors)
    return lax.all_to_all(current, "row", split_axis=0, concat_axis=1, tiled=True)


LITTLE = pl.CostEstimate(flops=1, bytes_accessed=1, transcendentals=0)
NT = (((1,), (1,)), ((), ()))
NN = (((1,), (0,)), ((), ()))


def split(value):
    high = value.astype(jnp.bfloat16)
    return high, (value - high.astype(jnp.float32)).astype(jnp.bfloat16)


def dot3(left, right, dims):
    def part(a, b):
        return lax.dot_general(a, b, dims, preferred_element_type=jnp.float32)

    return part(left[0], right[0]) + (part(left[0], right[1]) + part(left[1], right[0]))


def fdot(left, right, dims=NN):
    return dot3(split(left), split(right), dims)


def call(kernel, out_shape, *operands, scratch=(), limit=16):
    return pl.pallas_call(
        kernel,
        out_shape=out_shape,
        in_specs=[pl.BlockSpec(memory_space=pltpu.SMEM)]
        + [pl.BlockSpec(memory_space=pltpu.VMEM)] * (len(operands) - 1),
        out_specs=jax.tree.map(lambda _: pl.BlockSpec(memory_space=pltpu.VMEM), out_shape),
        scratch_shapes=list(scratch),
        cost_estimate=LITTLE,
        compiler_params=pltpu.CompilerParams(vmem_limit_bytes=limit * 2**20),
    )(*operands)


def own_rows(place, x, part):
    return pl.multiple_of(place[0] * (B // 2) + (place[1] ^ x) * part, part)


def place_rows(chips, place, dest, index, ref, begin, sib, sib_begin):
    part = B // 2 // chips
    for x in range(chips):
        at = pl.multiple_of(place[0] * (B // 2) + (place[1] ^ x) * part, part)
        dest[index, pl.ds(at, part), :] = ref[x, begin : begin + part]
        at = pl.multiple_of((1 - place[0]) * (B // 2) + (place[1] ^ x) * part, part)
        dest[index, pl.ds(at, part), :] = sib[x, sib_begin : sib_begin + part]


def product_kernel(chips, plan, choice, lefts, place, *refs):
    e_ref, out_ref, kept = refs[0], refs[-5], refs[-4:]
    groups, at = [], 1
    while at < len(refs) - 5:
        size = 4 if len(groups) == choice else 2
        groups.append(refs[at : at + size])
        at += size
    edge = place[2] == 1
    width = e_ref.shape[1] // 2
    step = min(width, 512)
    mine = e_ref.shape[0] // chips
    part = B // 2 // chips

    def read(slot, h, rows, cols):
        group = groups[slot]
        if len(group) == 2:
            return group[h][rows, cols]
        return jnp.where(edge, group[h][rows, cols], group[2 + h][rows, cols])

    totals = [None] * len(plan)
    for h in range(2):
        for k in range(0, width, step):
            at = pl.multiple_of((place[0] ^ h) * width + k, step)
            cols = slice(k, k + step)
            left = [e_ref[:, pl.ds(at, step)]]
            for j in range(lefts):
                left += [read(j, h, pl.ds(own_rows(place, x, part), part), cols) for x in range(chips)]
            both = split(jnp.concatenate(left))
            for i, (target, used) in enumerate(plan):
                rows = chips * mine + used * (B // 2)
                right = split(read(target, h, slice(None), cols))
                for ref, value in zip(kept[2 * h : 2 * h + 2], right):
                    ref[i * B : (i + 1) * B, cols] = value
                value = dot3(tuple(b[:rows] for b in both), right, NT)
                totals[i] = value if totals[i] is None else totals[i] + value
    begin = 0
    for value in totals:
        for x in range(chips):
            out_ref[x, begin : begin + mine] = value[x * mine : (x + 1) * mine]
        begin += mine
    for (_, used), value in zip(plan, totals):
        for j in range(used):
            for x in range(chips):
                at = chips * mine + j * (B // 2) + x * part
                out_ref[x, begin : begin + part] = value[at : at + part]
            begin += part


def inverse_kernel(chips, mine, place, f01, f2, fb, s01, s2, sb, out_ref, g_ref, high_ref, low_ref, gram_ref):
    part = B // 2 // chips

    def stored(dest, index, ref, at, sib):
        place_rows(chips, place, dest, index, ref, at * part + (2 * mine if ref is f01 else mine if ref is f2 else 0), sib, at * part)

    for slot, (ref, at, sib) in enumerate(((f01, 0, s01), (f01, 2, s01), (f2, 2, s2), (fb, 2, sb))):
        stored(gram_ref, slot, ref, at, sib)
    pairs = ((f01, 1, s01), (f2, 0, s2), (f2, 1, s2), (fb, 1, sb), (fb, 0, sb), (fb, 3, sb), (f2, 3, s2))
    for index, (ref, at, sib) in enumerate(pairs):
        stored(g_ref, index, ref, at, sib)
    for slot, value in enumerate((f01[:, :mine], f01[:, mine : 2 * mine], f2[:, :mine])):
        high, low = split(value.reshape(chips * mine, B))
        high_ref[:, slot * B : (slot + 1) * B] = high
        low_ref[:, slot * B : (slot + 1) * B] = low
    half = B // 2
    rows = lax.broadcasted_iota(jnp.int32, (half, half), 0)
    cols = lax.broadcasted_iota(jnp.int32, (half, half), 1)
    grams = [gram_ref[i, k : k + half, k : k + half] for i in range(PANELS) for k in (0, half)]
    inv = [jnp.where(rows == cols, 2.0 / gram, 0.0) for gram in grams]
    size = 1
    while size < half:
        pick = (rows // (2 * size) == cols // (2 * size)) & (rows % (2 * size) >= size) & (cols % (2 * size) < size)
        inner = [fdot(i, jnp.where(pick, gram, 0.0)) for i, gram in zip(inv, grams)]
        inv = [i - fdot(t, i) for i, t in zip(inv, inner)]
        size *= 2
    for i in range(PANELS):
        first, second = inv[2 * i], inv[2 * i + 1]
        out_ref[i, :half, :half] = first
        out_ref[i, :half, half:] = jnp.zeros((half, half), jnp.float32)
        out_ref[i, half:, :half] = -fdot(fdot(second, gram_ref[i, half:, :half]), first)
        out_ref[i, half:, half:] = second


def combine_kernel(place, t_ref, g_ref, high_ref, low_ref):
    edge, c = place[2], place[3]
    lower, inverses, whole = {}, {}, {}
    for which in range(PANELS):
        inverses[which] = t_ref[c ^ which]
        whole[which, which] = split(inverses[which])
        for later in range(which + 1, PANELS):
            slot, other = c ^ which, c ^ later
            low, high = jnp.minimum(slot, other), jnp.maximum(slot, other)
            turned = jnp.where((low == 2) & (edge == 0), 1, 0)
            gram = g_ref[high * (high - 1) // 2 + low + turned]
            row_slot = jnp.where(turned == 1, high, low)
            lower[later, which] = jnp.where(other == row_slot, gram, gram.T)
    for which in reversed(range(PANELS - 1)):
        scaled = [fdot(lower[r, which], inverses[which]) for r in range(which + 1, PANELS)]
        scaled = [split(s) for s in scaled]
        for later in range(which + 1, PANELS):
            value = None
            for r in range(which + 1, later + 1):
                term = dot3(whole[later, r], scaled[r - which - 1], NN)
                value = term if value is None else value + term
            whole[later, which] = split(-value)
    zeros = jnp.zeros((B, B), jnp.bfloat16)
    for q in range(PANELS):
        for p in range(PANELS):
            high, low = whole.get((q, p), (zeros, zeros))
            rows = pl.ds(pl.multiple_of((c ^ q) * B, B), B)
            cols = pl.ds(pl.multiple_of((c ^ p) * B, B), B)
            high_ref[rows, cols] = high
            low_ref[rows, cols] = low


def apply_kernel(chips, mine, place, p_high, p_low, f3, m_high, m_low, high_ref, low_ref):
    early = (PANELS - 1) * B
    solved = dot3((p_high[...], p_low[...]), (m_high[:early], m_low[:early]), NN)
    solved = solved + dot3(split(f3[...].reshape(chips * mine, B)), (m_high[early:], m_low[early:]), NN)
    high_ref[...], low_ref[...] = split(solved)


def update_kernel(chips, half, place, e_ref, s_high, s_low, *refs):
    out_ref = refs[-1]
    width = out_ref.shape[-1]
    mine = out_ref.shape[1]
    step = min(width, 512)
    for k in range(0, width, step):
        at = pl.multiple_of((place[0] ^ half) * width + k, step)
        value = e_ref[:, pl.ds(at, step)]
        begin = 0
        for high, low in zip(refs[:-1:2], refs[1:-1:2]):
            rows = slice(begin, begin + high.shape[0])
            begin += high.shape[0]
            cols = slice(k, k + step)
            value = value - dot3((s_high[:, rows], s_low[:, rows]), (high[:, cols], low[:, cols]), NN)
        out_ref[:, :, k : k + step] = value.reshape(chips, mine, step)


def panels_on_cols(eigvecs, reflectors, chips):
    width = reflectors.shape[1]
    r, c = lax.axis_index("row"), lax.axis_index("col")
    core, chip = r % 2, r // 2
    edge = (c == 0) | (c == 3)
    place = jnp.stack([core, chip, edge, c]).astype(jnp.int32)
    mine = eigvecs.shape[0]
    part = B // 2 // chips
    f32 = lambda *shape: jax.ShapeDtypeStruct(shape, jnp.float32)
    b16 = lambda *shape: jax.ShapeDtypeStruct(shape, jnp.bfloat16)

    def across(value, x):
        return lax.ppermute(value, "row", [(i, i ^ (2 * x)) for i in range(2 * chips)])

    def sibling(value):
        return lax.ppermute(value, "row", [(i, i ^ 1) for i in range(2 * chips)])

    def zmove(value, pairs):
        return lax.ppermute(value, "col", pairs)

    def scatter(packed):
        held = packed[0]
        for x in range(1, chips):
            held = held + across(packed[x], x)
        return held

    def collect(held):
        return jnp.stack([held] + [across(held, x) for x in range(1, chips)])

    def products(plan, choice, lefts, *operands):
        rows = sum(mine + used * part for _, used in plan)
        kernel = functools.partial(product_kernel, chips, plan, choice, lefts)
        kept = b16(len(plan) * B, width)
        return call(kernel, (f32(chips, rows, B), kept, kept, kept, kept), place, grid, *operands, limit=40)

    vectors = masked_vectors(reflectors, c, r * width)
    vectors, eigvecs = lax.optimization_barrier((vectors, eigvecs))
    near = zmove(vectors, [(0, 1), (1, 0), (2, 3), (3, 2)])
    inner = zmove(vectors, [(1, 2), (2, 1)])
    pieces = [lax.dynamic_slice(eigvecs, (0, (chip ^ x) * 2 * width), (mine, 2 * width)) for x in range(chips)]
    grid = jnp.concatenate(pieces[:1] + [across(pieces[x], x) for x in range(1, chips)])
    grid, near, inner, vectors = lax.optimization_barrier((grid, near, inner, vectors))

    second_out = zmove(inner, [(1, 0), (2, 3)])
    second_in = zmove(near, [(1, 2), (2, 1)])
    zero, one = (vectors, sibling(vectors)), (near, sibling(near))
    packed_01, *kept_01 = products(((0, 1), (1, 2)), -1, 2, *zero, *one)
    held_01 = scatter(packed_01)
    from_01 = [across(held_01, x) for x in range(1, chips)]
    second_out, second_in, from_01[0] = lax.optimization_barrier((second_out, second_in, from_01[0]))

    third_out = zmove(second_in, [(1, 0), (2, 3)])
    two = (second_out, sibling(second_out), second_in, sibling(second_in))
    full_01 = jnp.stack([held_01] + from_01)
    inner_o = sibling(inner)
    packed_2, *kept_2 = products(((2, 4),), 2, 4, *zero, *one, *two, inner, inner_o)
    held_2 = scatter(packed_2)
    partner = zmove(held_2[mine:], [(0, 1), (1, 0), (2, 3), (3, 2)])
    full_2 = collect(held_2)
    sib_01 = sibling(full_01[:, 2 * mine :])
    third_out, full_01, sib_01, full_2, partner = lax.optimization_barrier((third_out, full_01, sib_01, full_2, partner))

    third_o, full_2 = lax.optimization_barrier((sibling(third_out), full_2))
    packed_3, *kept_3 = products(((0, 0),), 0, 0, third_out, third_o, inner, inner_o)
    from_b = [across(partner, x) for x in range(1, chips)]
    from_b, _ = lax.optimization_barrier((from_b, packed_3))
    full_b = jnp.stack([partner] + from_b)
    sib_2, sib_b = sibling(full_2[:, mine:]), sibling(full_b)
    early = b16(chips * mine, (PANELS - 1) * B)
    inverses, grams, *p_early = call(
        functools.partial(inverse_kernel, chips, mine),
        (f32(PANELS, B, B), f32(7, B, B), early, early),
        place,
        *(full_01, full_2, full_b, sib_01, sib_2, sib_b),
        scratch=[pltpu.VMEM((PANELS, B, B), jnp.float32)],
        limit=24,
    )
    from_3 = [across(packed_3[x], x) for x in range(1, chips)]
    from_3, inverses = lax.optimization_barrier((from_3, inverses))
    held_3 = sum(from_3, packed_3[0])
    whole = b16(PANELS * B, PANELS * B)
    inverse = call(combine_kernel, (whole, whole), place, inverses, grams, limit=32)
    from_3 = [across(held_3, x) for x in range(1, chips)]
    from_3, inverse = lax.optimization_barrier((from_3, inverse))
    full_3 = jnp.stack([held_3] + from_3)
    solved = b16(chips * mine, PANELS * B)
    solved = call(
        functools.partial(apply_kernel, chips, mine), (solved, solved), place, *p_early, full_3, *inverse, limit=24
    )
    result = jnp.zeros_like(eigvecs)
    for half in range(2):
        done = call(
            functools.partial(update_kernel, chips, half),
            f32(chips, mine, width),
            place,
            *(grid, *solved),
            *(kept_01[2 * half : 2 * half + 2] + kept_2[2 * half : 2 * half + 2] + kept_3[2 * half : 2 * half + 2]),
            limit=32,
        )
        for x in range(chips):
            piece = across(done[x], x) if x else done[x]
            start = (chip ^ x) * 2 * width + (core ^ half) * width
            result = lax.dynamic_update_slice(result, piece, (0, start))
    return result


def solution(mesh):
    rows, cols = mesh.shape["row"], mesh.shape["col"]
    placed = (P(("row", "col"), None), P("col", "row"))

    def shards(eigvecs, reflectors):
        if cols == PANELS and reflectors.shape[0] == B and rows >= 4 and rows & (rows - 1) == 0 and B % (16 * rows) == 0:
            return panels_on_cols(eigvecs, reflectors, rows // 2)
        return general(eigvecs, reflectors)

    return jax.shard_map(shards, mesh=mesh, in_specs=placed, out_specs=P(("row", "col"), None), check_vma=False)
```

```python
import functools

import jax
import jax.numpy as jnp
from jax import lax
from jax.experimental import pallas as pl
from jax.experimental.pallas import tpu as pltpu
from jax.sharding import PartitionSpec as P

B = 256
PANELS = 4


def masked_vectors(block, which, row_base):
    rows_all = lax.broadcasted_iota(jnp.int32, block.shape, 1) + row_base
    starts = lax.broadcasted_iota(jnp.int32, block.shape, 0) + which * B
    unit = jnp.where(rows_all == starts, jnp.ones_like(block), jnp.zeros_like(block))
    return jnp.where(rows_all > starts, block, unit)


def upper_factor(gram):
    return jnp.triu(gram, 1) + jnp.diag(jnp.diag(gram) * 0.5)


def hdot(left, right):
    return jnp.dot(left, right, precision=lax.Precision.HIGHEST, preferred_element_type=jnp.float32)


def apply_inverse(product, factor):
    order = factor.shape[0]
    diagonal = jnp.diagonal(factor)
    nilpotent = -jnp.triu(factor, 1) / diagonal[:, None]
    solved = product / diagonal[None, :]
    power = nilpotent
    solved = solved + hdot(solved, power.T)
    for level in range((order - 1).bit_length() - 1):
        power = hdot(power, power)
        solved = solved + hdot(solved, power.T)
    return solved


def general(eigvecs, reflectors):
    current = lax.all_to_all(eigvecs, "row", split_axis=1, concat_axis=0, tiled=True)
    gathered = lax.all_gather(reflectors, "col", axis=0, tiled=True)
    local_rows = current.shape[1]
    row_base = lax.axis_index("row") * local_rows
    blocks = []
    for which in range(PANELS):
        blocks.append(masked_vectors(gathered[which * B : (which + 1) * B, :], which, row_base))
    gram_local = jnp.stack([hdot(vectors, vectors.T) for vectors in blocks])
    gram_all = lax.psum(gram_local, "row")
    for which in reversed(range(PANELS)):
        vectors = blocks[which]
        factor = upper_factor(gram_all[which])
        partial_value = hdot(current, vectors.T)
        summed = lax.psum(partial_value, "row")
        solved = apply_inverse(summed, factor)
        current = current - hdot(solved, vectors)
    return lax.all_to_all(current, "row", split_axis=0, concat_axis=1, tiled=True)


LITTLE = pl.CostEstimate(flops=1, bytes_accessed=1, transcendentals=0)
NT = (((1,), (1,)), ((), ()))
NN = (((1,), (0,)), ((), ()))


def split(value):
    high = value.astype(jnp.bfloat16)
    return high, (value - high.astype(jnp.float32)).astype(jnp.bfloat16)


def dot3(left, right, dims):
    def part(a, b):
        return lax.dot_general(a, b, dims, preferred_element_type=jnp.float32)

    return part(left[0], right[0]) + (part(left[0], right[1]) + part(left[1], right[0]))


def fdot(left, right, dims=NN):
    return dot3(split(left), split(right), dims)


def call(kernel, out_shape, *operands, scratch=(), limit=16):
    return pl.pallas_call(
        kernel,
        out_shape=out_shape,
        in_specs=[pl.BlockSpec(memory_space=pltpu.SMEM)]
        + [pl.BlockSpec(memory_space=pltpu.VMEM)] * (len(operands) - 1),
        out_specs=jax.tree.map(lambda _: pl.BlockSpec(memory_space=pltpu.VMEM), out_shape),
        scratch_shapes=list(scratch),
        cost_estimate=LITTLE,
        compiler_params=pltpu.CompilerParams(vmem_limit_bytes=limit * 2**20),
    )(*operands)


def own_rows(place, x, part):
    return pl.multiple_of(place[0] * (B // 2) + (place[1] ^ x) * part, part)


def place_rows(chips, place, dest, index, ref, begin, sib, sib_begin):
    part = B // 2 // chips
    for x in range(chips):
        at = pl.multiple_of(place[0] * (B // 2) + (place[1] ^ x) * part, part)
        dest[index, pl.ds(at, part), :] = ref[x, begin : begin + part]
        at = pl.multiple_of((1 - place[0]) * (B // 2) + (place[1] ^ x) * part, part)
        dest[index, pl.ds(at, part), :] = sib[x, sib_begin : sib_begin + part]


def product_kernel(chips, plan, choice, lefts, place, *refs):
    e_ref, out_ref, kept = refs[0], refs[-5], refs[-4:]
    groups, at = [], 1
    while at < len(refs) - 5:
        size = 4 if len(groups) == choice else 2
        groups.append(refs[at : at + size])
        at += size
    edge = place[2] == 1
    width = e_ref.shape[1] // 2
    step = min(width, 512)
    mine = e_ref.shape[0] // chips
    part = B // 2 // chips

    def read(slot, h, rows, cols):
        group = groups[slot]
        if len(group) == 2:
            return group[h][rows, cols]
        return jnp.where(edge, group[h][rows, cols], group[2 + h][rows, cols])

    totals = [None] * len(plan)
    for h in range(2):
        for k in range(0, width, step):
            at = pl.multiple_of((place[0] ^ h) * width + k, step)
            cols = slice(k, k + step)
            left = [e_ref[:, pl.ds(at, step)]]
            for j in range(lefts):
                left += [read(j, h, pl.ds(own_rows(place, x, part), part), cols) for x in range(chips)]
            both = split(jnp.concatenate(left))
            for i, (target, used) in enumerate(plan):
                rows = chips * mine + used * (B // 2)
                right = split(read(target, h, slice(None), cols))
                for ref, value in zip(kept[2 * h : 2 * h + 2], right):
                    ref[i * B : (i + 1) * B, cols] = value
                value = dot3(tuple(b[:rows] for b in both), right, NT)
                totals[i] = value if totals[i] is None else totals[i] + value
    begin = 0
    for value in totals:
        for x in range(chips):
            out_ref[x, begin : begin + mine] = value[x * mine : (x + 1) * mine]
        begin += mine
    for (_, used), value in zip(plan, totals):
        for j in range(used):
            for x in range(chips):
                at = chips * mine + j * (B // 2) + x * part
                out_ref[x, begin : begin + part] = value[at : at + part]
            begin += part


def inverse_kernel(chips, mine, place, f01, f2, fb, s01, s2, sb, out_ref, g_ref, high_ref, low_ref, gram_ref):
    part = B // 2 // chips

    def stored(dest, index, ref, at, sib):
        place_rows(chips, place, dest, index, ref, at * part + (2 * mine if ref is f01 else mine if ref is f2 else 0), sib, at * part)

    for slot, (ref, at, sib) in enumerate(((f01, 0, s01), (f01, 2, s01), (f2, 2, s2), (fb, 2, sb))):
        stored(gram_ref, slot, ref, at, sib)
    pairs = ((f01, 1, s01), (f2, 0, s2), (f2, 1, s2), (fb, 1, sb), (fb, 0, sb), (fb, 3, sb), (f2, 3, s2))
    for index, (ref, at, sib) in enumerate(pairs):
        stored(g_ref, index, ref, at, sib)
    for slot, value in enumerate((f01[:, :mine], f01[:, mine : 2 * mine], f2[:, :mine])):
        high, low = split(value.reshape(chips * mine, B))
        high_ref[:, slot * B : (slot + 1) * B] = high
        low_ref[:, slot * B : (slot + 1) * B] = low
    half = B // 2
    rows = lax.broadcasted_iota(jnp.int32, (half, half), 0)
    cols = lax.broadcasted_iota(jnp.int32, (half, half), 1)
    grams = [gram_ref[i, k : k + half, k : k + half] for i in range(PANELS) for k in (0, half)]
    inv = [jnp.where(rows == cols, 2.0 / gram, 0.0) for gram in grams]
    size = 1
    while size < half:
        pick = (rows // (2 * size) == cols // (2 * size)) & (rows % (2 * size) >= size) & (cols % (2 * size) < size)
        inner = [fdot(i, jnp.where(pick, gram, 0.0)) for i, gram in zip(inv, grams)]
        inv = [i - fdot(t, i) for i, t in zip(inv, inner)]
        size *= 2
    for i in range(PANELS):
        first, second = inv[2 * i], inv[2 * i + 1]
        out_ref[i, :half, :half] = first
        out_ref[i, :half, half:] = jnp.zeros((half, half), jnp.float32)
        out_ref[i, half:, :half] = -fdot(fdot(second, gram_ref[i, half:, :half]), first)
        out_ref[i, half:, half:] = second


def combine_kernel(place, t_ref, g_ref, high_ref, low_ref):
    edge, c = place[2], place[3]
    lower, inverses, whole = {}, {}, {}
    for which in range(PANELS):
        inverses[which] = t_ref[c ^ which]
        whole[which, which] = split(inverses[which])
        for later in range(which + 1, PANELS):
            slot, other = c ^ which, c ^ later
            low, high = jnp.minimum(slot, other), jnp.maximum(slot, other)
            turned = jnp.where((low == 2) & (edge == 0), 1, 0)
            gram = g_ref[high * (high - 1) // 2 + low + turned]
            row_slot = jnp.where(turned == 1, high, low)
            lower[later, which] = jnp.where(other == row_slot, gram, gram.T)
    for which in reversed(range(PANELS - 1)):
        scaled = [fdot(lower[r, which], inverses[which]) for r in range(which + 1, PANELS)]
        scaled = [split(s) for s in scaled]
        for later in range(which + 1, PANELS):
            value = None
            for r in range(which + 1, later + 1):
                term = dot3(whole[later, r], scaled[r - which - 1], NN)
                value = term if value is None else value + term
            whole[later, which] = split(-value)
    zeros = jnp.zeros((B, B), jnp.bfloat16)
    for q in range(PANELS):
        for p in range(PANELS):
            high, low = whole.get((q, p), (zeros, zeros))
            rows = pl.ds(pl.multiple_of((c ^ q) * B, B), B)
            cols = pl.ds(pl.multiple_of((c ^ p) * B, B), B)
            high_ref[rows, cols] = high
            low_ref[rows, cols] = low


def apply_kernel(place, p_high, p_low, m_high, m_low, *refs):
    early = (PANELS - 1) * B
    solved = dot3((p_high[...], p_low[...]), (m_high[:early], m_low[:early]), NN)
    last = jnp.concatenate([ref[...] for ref in refs[:-2]])
    solved = solved + dot3(split(last), (m_high[early:], m_low[early:]), NN)
    refs[-2][...], refs[-1][...] = split(solved)


def update_kernel(chips, half, place, e_ref, s_high, s_low, *refs):
    out_ref = refs[-1]
    width = out_ref.shape[-1]
    mine = out_ref.shape[1]
    step = min(width, 512)
    for k in range(0, width, step):
        at = pl.multiple_of((place[0] ^ half) * width + k, step)
        value = e_ref[:, pl.ds(at, step)]
        begin = 0
        for high, low in zip(refs[:-1:2], refs[1:-1:2]):
            rows = slice(begin, begin + high.shape[0])
            begin += high.shape[0]
            cols = slice(k, k + step)
            value = value - dot3((s_high[:, rows], s_low[:, rows]), (high[:, cols], low[:, cols]), NN)
        out_ref[:, :, k : k + step] = value.reshape(chips, mine, step)


def panels_on_cols(eigvecs, reflectors, chips):
    width = reflectors.shape[1]
    r, c = lax.axis_index("row"), lax.axis_index("col")
    core, chip = r % 2, r // 2
    edge = (c == 0) | (c == 3)
    place = jnp.stack([core, chip, edge, c]).astype(jnp.int32)
    mine = eigvecs.shape[0]
    part = B // 2 // chips
    f32 = lambda *shape: jax.ShapeDtypeStruct(shape, jnp.float32)
    b16 = lambda *shape: jax.ShapeDtypeStruct(shape, jnp.bfloat16)

    def across(value, x):
        return lax.ppermute(value, "row", [(i, i ^ (2 * x)) for i in range(2 * chips)])

    def sibling(value):
        return lax.ppermute(value, "row", [(i, i ^ 1) for i in range(2 * chips)])

    def zmove(value, pairs):
        return lax.ppermute(value, "col", pairs)

    def scatter(packed):
        held = packed[0]
        for x in range(1, chips):
            held = held + across(packed[x], x)
        return held

    def collect(held):
        return jnp.stack([held] + [across(held, x) for x in range(1, chips)])

    def products(plan, choice, lefts, *operands):
        rows = sum(mine + used * part for _, used in plan)
        kernel = functools.partial(product_kernel, chips, plan, choice, lefts)
        kept = b16(len(plan) * B, width)
        return call(kernel, (f32(chips, rows, B), kept, kept, kept, kept), place, grid, *operands, limit=24)

    vectors = masked_vectors(reflectors, c, r * width)
    vectors, eigvecs = lax.optimization_barrier((vectors, eigvecs))
    near = zmove(vectors, [(0, 1), (1, 0), (2, 3), (3, 2)])
    inner = zmove(vectors, [(1, 2), (2, 1)])
    pieces = [lax.dynamic_slice(eigvecs, (0, (chip ^ x) * 2 * width), (mine, 2 * width)) for x in range(chips)]
    grid = jnp.concatenate(pieces[:1] + [across(pieces[x], x) for x in range(1, chips)])
    grid, near, inner, vectors = lax.optimization_barrier((grid, near, inner, vectors))

    second_out = zmove(inner, [(1, 0), (2, 3)])
    second_in = zmove(near, [(1, 2), (2, 1)])
    zero, one = (vectors, sibling(vectors)), (near, sibling(near))
    packed_01, *kept_01 = products(((0, 1), (1, 2)), -1, 2, *zero, *one)
    held_01 = scatter(packed_01)
    from_01 = [across(held_01, x) for x in range(1, chips)]
    second_out, second_in, from_01[0] = lax.optimization_barrier((second_out, second_in, from_01[0]))

    third_out = zmove(second_in, [(1, 0), (2, 3)])
    two = (second_out, sibling(second_out), second_in, sibling(second_in))
    full_01 = jnp.stack([held_01] + from_01)
    inner_o = sibling(inner)
    packed_2, *kept_2 = products(((2, 4),), 2, 4, *zero, *one, *two, inner, inner_o)
    held_2 = scatter(packed_2)
    partner = zmove(held_2[mine:], [(0, 1), (1, 0), (2, 3), (3, 2)])
    full_2 = collect(held_2)
    sib_01 = sibling(full_01[:, 2 * mine :])
    third_out, full_01, sib_01, full_2, partner = lax.optimization_barrier((third_out, full_01, sib_01, full_2, partner))

    third_o, full_2 = lax.optimization_barrier((sibling(third_out), full_2))
    packed_3, *kept_3 = products(((0, 0),), 0, 0, third_out, third_o, inner, inner_o)
    from_b = [across(partner, x) for x in range(1, chips)]
    from_b, _ = lax.optimization_barrier((from_b, packed_3))
    full_b = jnp.stack([partner] + from_b)
    sib_2, sib_b = sibling(full_2[:, mine:]), sibling(full_b)
    early = b16(chips * mine, (PANELS - 1) * B)
    inverses, grams, *p_early = call(
        functools.partial(inverse_kernel, chips, mine),
        (f32(PANELS, B, B), f32(7, B, B), early, early),
        place,
        *(full_01, full_2, full_b, sib_01, sib_2, sib_b),
        scratch=[pltpu.VMEM((PANELS, B, B), jnp.float32)],
        limit=16,
    )
    from_3 = [across(packed_3[x], x) for x in range(1, chips)]
    from_3, inverses = lax.optimization_barrier((from_3, inverses))
    held_3 = sum(from_3, packed_3[0])
    whole = b16(PANELS * B, PANELS * B)
    inverse = call(combine_kernel, (whole, whole), place, inverses, grams, limit=16)
    from_3 = [across(held_3, x) for x in range(1, chips)]
    from_3, inverse = lax.optimization_barrier((from_3, inverse))
    solved = b16(chips * mine, PANELS * B)
    solved = call(
        apply_kernel, (solved, solved), place, *p_early, *inverse, held_3, *from_3, limit=16
    )
    result = jnp.zeros_like(eigvecs)
    for half in range(2):
        done = call(
            functools.partial(update_kernel, chips, half),
            f32(chips, mine, width),
            place,
            *(grid, *solved),
            *(kept_01[2 * half : 2 * half + 2] + kept_2[2 * half : 2 * half + 2] + kept_3[2 * half : 2 * half + 2]),
            limit=20,
        )
        for x in range(chips):
            piece = across(done[x], x) if x else done[x]
            start = (chip ^ x) * 2 * width + (core ^ half) * width
            result = lax.dynamic_update_slice(result, piece, (0, start))
    return result


def solution(mesh):
    rows, cols = mesh.shape["row"], mesh.shape["col"]
    placed = (P(("row", "col"), None), P("col", "row"))

    def shards(eigvecs, reflectors):
        if cols == PANELS and reflectors.shape[0] == B and rows >= 4 and rows & (rows - 1) == 0 and B % (16 * rows) == 0:
            return panels_on_cols(eigvecs, reflectors, rows // 2)
        return general(eigvecs, reflectors)

    return jax.shard_map(shards, mesh=mesh, in_specs=placed, out_specs=P(("row", "col"), None), check_vma=False)
```

```python
import functools

import jax
import jax.numpy as jnp
from jax import lax
from jax.experimental import pallas as pl
from jax.experimental.pallas import tpu as pltpu
from jax.sharding import PartitionSpec as P

B = 256
PANELS = 4


def masked_vectors(block, which, row_base):
    rows_all = lax.broadcasted_iota(jnp.int32, block.shape, 1) + row_base
    starts = lax.broadcasted_iota(jnp.int32, block.shape, 0) + which * B
    unit = jnp.where(rows_all == starts, jnp.ones_like(block), jnp.zeros_like(block))
    return jnp.where(rows_all > starts, block, unit)


def upper_factor(gram):
    return jnp.triu(gram, 1) + jnp.diag(jnp.diag(gram) * 0.5)


def hdot(left, right):
    return jnp.dot(left, right, precision=lax.Precision.HIGHEST, preferred_element_type=jnp.float32)


def apply_inverse(product, factor):
    order = factor.shape[0]
    diagonal = jnp.diagonal(factor)
    nilpotent = -jnp.triu(factor, 1) / diagonal[:, None]
    solved = product / diagonal[None, :]
    power = nilpotent
    solved = solved + hdot(solved, power.T)
    for level in range((order - 1).bit_length() - 1):
        power = hdot(power, power)
        solved = solved + hdot(solved, power.T)
    return solved


def general(eigvecs, reflectors):
    current = lax.all_to_all(eigvecs, "row", split_axis=1, concat_axis=0, tiled=True)
    gathered = lax.all_gather(reflectors, "col", axis=0, tiled=True)
    local_rows = current.shape[1]
    row_base = lax.axis_index("row") * local_rows
    blocks = []
    for which in range(PANELS):
        blocks.append(masked_vectors(gathered[which * B : (which + 1) * B, :], which, row_base))
    gram_local = jnp.stack([hdot(vectors, vectors.T) for vectors in blocks])
    gram_all = lax.psum(gram_local, "row")
    for which in reversed(range(PANELS)):
        vectors = blocks[which]
        factor = upper_factor(gram_all[which])
        partial_value = hdot(current, vectors.T)
        summed = lax.psum(partial_value, "row")
        solved = apply_inverse(summed, factor)
        current = current - hdot(solved, vectors)
    return lax.all_to_all(current, "row", split_axis=0, concat_axis=1, tiled=True)


LITTLE = pl.CostEstimate(flops=1, bytes_accessed=1, transcendentals=0)
NT = (((1,), (1,)), ((), ()))
NN = (((1,), (0,)), ((), ()))


def split(value):
    high = value.astype(jnp.bfloat16)
    return high, (value - high.astype(jnp.float32)).astype(jnp.bfloat16)


def dot3(left, right, dims):
    def part(a, b):
        return lax.dot_general(a, b, dims, preferred_element_type=jnp.float32)

    return part(left[0], right[0]) + (part(left[0], right[1]) + part(left[1], right[0]))


def fdot(left, right, dims=NN):
    return dot3(split(left), split(right), dims)


def call(kernel, out_shape, *operands, scratch=(), limit=16):
    return pl.pallas_call(
        kernel,
        out_shape=out_shape,
        in_specs=[pl.BlockSpec(memory_space=pltpu.SMEM)]
        + [pl.BlockSpec(memory_space=pltpu.VMEM)] * (len(operands) - 1),
        out_specs=jax.tree.map(lambda _: pl.BlockSpec(memory_space=pltpu.VMEM), out_shape),
        scratch_shapes=list(scratch),
        cost_estimate=LITTLE,
        compiler_params=pltpu.CompilerParams(vmem_limit_bytes=limit * 2**20),
    )(*operands)


def own_rows(place, x, part):
    return pl.multiple_of(place[0] * (B // 2) + (place[1] ^ x) * part, part)


def place_rows(chips, place, dest, index, ref, begin, sib, sib_begin):
    part = B // 2 // chips
    for x in range(chips):
        at = pl.multiple_of(place[0] * (B // 2) + (place[1] ^ x) * part, part)
        dest[index, pl.ds(at, part), :] = ref[x, begin : begin + part]
        at = pl.multiple_of((1 - place[0]) * (B // 2) + (place[1] ^ x) * part, part)
        dest[index, pl.ds(at, part), :] = sib[x, sib_begin : sib_begin + part]


def product_kernel(chips, plan, choice, lefts, place, *refs):
    e_ref, out_ref, kept = refs[0], refs[-5], refs[-4:]
    groups, at = [], 1
    while at < len(refs) - 5:
        size = 4 if len(groups) == choice else 2
        groups.append(refs[at : at + size])
        at += size
    edge = place[2] == 1
    width = e_ref.shape[1] // 2
    step = min(width, 512)
    mine = e_ref.shape[0] // chips
    part = B // 2 // chips

    def read(slot, h, rows, cols):
        group = groups[slot]
        if len(group) == 2:
            return group[h][rows, cols]
        return jnp.where(edge, group[h][rows, cols], group[2 + h][rows, cols])

    totals = [None] * len(plan)
    for h in range(2):
        for k in range(0, width, step):
            at = pl.multiple_of((place[0] ^ h) * width + k, step)
            cols = slice(k, k + step)
            left = [e_ref[:, pl.ds(at, step)]]
            for j in range(lefts):
                left += [read(j, h, pl.ds(own_rows(place, x, part), part), cols) for x in range(chips)]
            both = split(jnp.concatenate(left))
            for i, (target, used) in enumerate(plan):
                rows = chips * mine + used * (B // 2)
                right = split(read(target, h, slice(None), cols))
                for ref, value in zip(kept[2 * h : 2 * h + 2], right):
                    ref[i * B : (i + 1) * B, cols] = value
                value = dot3(tuple(b[:rows] for b in both), right, NT)
                totals[i] = value if totals[i] is None else totals[i] + value
    begin = 0
    for value in totals:
        for x in range(chips):
            out_ref[x, begin : begin + mine] = value[x * mine : (x + 1) * mine]
        begin += mine
    for (_, used), value in zip(plan, totals):
        for j in range(used):
            for x in range(chips):
                at = chips * mine + j * (B // 2) + x * part
                out_ref[x, begin : begin + part] = value[at : at + part]
            begin += part


def inverse_kernel(chips, mine, place, f01, f2, fb, s01, s2, sb, out_ref, g_ref, high_ref, low_ref, gram_ref):
    part = B // 2 // chips

    def stored(dest, index, ref, at, sib):
        place_rows(chips, place, dest, index, ref, at * part + (2 * mine if ref is f01 else mine if ref is f2 else 0), sib, at * part)

    for slot, (ref, at, sib) in enumerate(((f01, 0, s01), (f01, 2, s01), (f2, 2, s2), (fb, 2, sb))):
        stored(gram_ref, slot, ref, at, sib)
    pairs = ((f01, 1, s01), (f2, 0, s2), (f2, 1, s2), (fb, 1, sb), (fb, 0, sb), (fb, 3, sb), (f2, 3, s2))
    for index, (ref, at, sib) in enumerate(pairs):
        stored(g_ref, index, ref, at, sib)
    for slot, value in enumerate((f01[:, :mine], f01[:, mine : 2 * mine], f2[:, :mine])):
        high, low = split(value.reshape(chips * mine, B))
        high_ref[:, slot * B : (slot + 1) * B] = high
        low_ref[:, slot * B : (slot + 1) * B] = low
    half = B // 2
    rows = lax.broadcasted_iota(jnp.int32, (half, half), 0)
    cols = lax.broadcasted_iota(jnp.int32, (half, half), 1)
    grams = [gram_ref[i, k : k + half, k : k + half] for i in range(PANELS) for k in (0, half)]
    inv = [jnp.where(rows == cols, 2.0 / gram, 0.0) for gram in grams]
    size = 1
    while size < half:
        pick = (rows // (2 * size) == cols // (2 * size)) & (rows % (2 * size) >= size) & (cols % (2 * size) < size)
        inner = [fdot(i, jnp.where(pick, gram, 0.0)) for i, gram in zip(inv, grams)]
        inv = [i - fdot(t, i) for i, t in zip(inv, inner)]
        size *= 2
    for i in range(PANELS):
        first, second = inv[2 * i], inv[2 * i + 1]
        out_ref[i, :half, :half] = first
        out_ref[i, :half, half:] = jnp.zeros((half, half), jnp.float32)
        out_ref[i, half:, :half] = -fdot(fdot(second, gram_ref[i, half:, :half]), first)
        out_ref[i, half:, half:] = second


def combine_kernel(place, t_ref, g_ref, high_ref, low_ref):
    edge, c = place[2], place[3]
    lower, inverses, whole = {}, {}, {}
    for which in range(PANELS):
        inverses[which] = t_ref[c ^ which]
        whole[which, which] = split(inverses[which])
        for later in range(which + 1, PANELS):
            slot, other = c ^ which, c ^ later
            low, high = jnp.minimum(slot, other), jnp.maximum(slot, other)
            turned = jnp.where((low == 2) & (edge == 0), 1, 0)
            gram = g_ref[high * (high - 1) // 2 + low + turned]
            row_slot = jnp.where(turned == 1, high, low)
            lower[later, which] = jnp.where(other == row_slot, gram, gram.T)
    for which in reversed(range(PANELS - 1)):
        scaled = [fdot(lower[r, which], inverses[which]) for r in range(which + 1, PANELS)]
        scaled = [split(s) for s in scaled]
        for later in range(which + 1, PANELS):
            value = None
            for r in range(which + 1, later + 1):
                term = dot3(whole[later, r], scaled[r - which - 1], NN)
                value = term if value is None else value + term
            whole[later, which] = split(-value)
    zeros = jnp.zeros((B, B), jnp.bfloat16)
    for q in range(PANELS):
        for p in range(PANELS):
            high, low = whole.get((q, p), (zeros, zeros))
            rows = pl.ds(pl.multiple_of((c ^ q) * B, B), B)
            cols = pl.ds(pl.multiple_of((c ^ p) * B, B), B)
            high_ref[rows, cols] = high
            low_ref[rows, cols] = low


def apply_kernel(place, p_high, p_low, m_high, m_low, *refs):
    early = (PANELS - 1) * B
    solved = dot3((p_high[...], p_low[...]), (m_high[:early], m_low[:early]), NN)
    last = jnp.concatenate([ref[...] for ref in refs[:-2]])
    solved = solved + dot3(split(last), (m_high[early:], m_low[early:]), NN)
    refs[-2][...], refs[-1][...] = split(solved)


def update_kernel(chips, half, place, e_ref, s_high, s_low, *refs):
    out_ref = refs[-1]
    width = out_ref.shape[-1]
    mine = out_ref.shape[1]
    step = min(width, 512)
    for k in range(0, width, step):
        at = pl.multiple_of((place[0] ^ half) * width + k, step)
        value = e_ref[:, pl.ds(at, step)]
        begin = 0
        for high, low in zip(refs[:-1:2], refs[1:-1:2]):
            rows = slice(begin, begin + high.shape[0])
            begin += high.shape[0]
            cols = slice(k, k + step)
            value = value - dot3((s_high[:, rows], s_low[:, rows]), (high[:, cols], low[:, cols]), NN)
        out_ref[:, :, k : k + step] = value.reshape(chips, mine, step)


def first_kernel(chips, place, *refs):
    ins, (high_ref, low_ref, out_ref) = refs[:-3], refs[-3:]
    apply_kernel(place, *ins[: 4 + chips], high_ref, low_ref)
    update_kernel(chips, 0, place, ins[4 + chips], high_ref, low_ref, *ins[5 + chips :], out_ref)


def panels_on_cols(eigvecs, reflectors, chips):
    width = reflectors.shape[1]
    r, c = lax.axis_index("row"), lax.axis_index("col")
    core, chip = r % 2, r // 2
    edge = (c == 0) | (c == 3)
    place = jnp.stack([core, chip, edge, c]).astype(jnp.int32)
    mine = eigvecs.shape[0]
    part = B // 2 // chips
    f32 = lambda *shape: jax.ShapeDtypeStruct(shape, jnp.float32)
    b16 = lambda *shape: jax.ShapeDtypeStruct(shape, jnp.bfloat16)

    def across(value, x):
        return lax.ppermute(value, "row", [(i, i ^ (2 * x)) for i in range(2 * chips)])

    def sibling(value):
        return lax.ppermute(value, "row", [(i, i ^ 1) for i in range(2 * chips)])

    def zmove(value, pairs):
        return lax.ppermute(value, "col", pairs)

    def scatter(packed):
        held = packed[0]
        for x in range(1, chips):
            held = held + across(packed[x], x)
        return held

    def collect(held):
        return jnp.stack([held] + [across(held, x) for x in range(1, chips)])

    def products(plan, choice, lefts, *operands):
        rows = sum(mine + used * part for _, used in plan)
        kernel = functools.partial(product_kernel, chips, plan, choice, lefts)
        kept = b16(len(plan) * B, width)
        return call(kernel, (f32(chips, rows, B), kept, kept, kept, kept), place, grid, *operands, limit=24)

    vectors = masked_vectors(reflectors, c, r * width)
    vectors, eigvecs = lax.optimization_barrier((vectors, eigvecs))
    near = zmove(vectors, [(0, 1), (1, 0), (2, 3), (3, 2)])
    inner = zmove(vectors, [(1, 2), (2, 1)])
    pieces = [lax.dynamic_slice(eigvecs, (0, (chip ^ x) * 2 * width), (mine, 2 * width)) for x in range(chips)]
    grid = jnp.concatenate(pieces[:1] + [across(pieces[x], x) for x in range(1, chips)])
    grid, near, inner, vectors = lax.optimization_barrier((grid, near, inner, vectors))

    second_out = zmove(inner, [(1, 0), (2, 3)])
    second_in = zmove(near, [(1, 2), (2, 1)])
    zero, one = (vectors, sibling(vectors)), (near, sibling(near))
    packed_01, *kept_01 = products(((0, 1), (1, 2)), -1, 2, *zero, *one)
    held_01 = scatter(packed_01)
    from_01 = [across(held_01, x) for x in range(1, chips)]
    second_out, second_in, from_01[0] = lax.optimization_barrier((second_out, second_in, from_01[0]))

    third_out = zmove(second_in, [(1, 0), (2, 3)])
    two = (second_out, sibling(second_out), second_in, sibling(second_in))
    full_01 = jnp.stack([held_01] + from_01)
    inner_o = sibling(inner)
    packed_2, *kept_2 = products(((2, 4),), 2, 4, *zero, *one, *two, inner, inner_o)
    held_2 = scatter(packed_2)
    partner = zmove(held_2[mine:], [(0, 1), (1, 0), (2, 3), (3, 2)])
    full_2 = collect(held_2)
    sib_01 = sibling(full_01[:, 2 * mine :])
    third_out, full_01, sib_01, full_2, partner = lax.optimization_barrier((third_out, full_01, sib_01, full_2, partner))

    third_o, full_2 = lax.optimization_barrier((sibling(third_out), full_2))
    packed_3, *kept_3 = products(((0, 0),), 0, 0, third_out, third_o, inner, inner_o)
    from_b = [across(partner, x) for x in range(1, chips)]
    from_b, _ = lax.optimization_barrier((from_b, packed_3))
    full_b = jnp.stack([partner] + from_b)
    sib_2, sib_b = sibling(full_2[:, mine:]), sibling(full_b)
    early = b16(chips * mine, (PANELS - 1) * B)
    inverses, grams, *p_early = call(
        functools.partial(inverse_kernel, chips, mine),
        (f32(PANELS, B, B), f32(7, B, B), early, early),
        place,
        *(full_01, full_2, full_b, sib_01, sib_2, sib_b),
        scratch=[pltpu.VMEM((PANELS, B, B), jnp.float32)],
        limit=16,
    )
    from_3 = [across(packed_3[x], x) for x in range(1, chips)]
    from_3, inverses = lax.optimization_barrier((from_3, inverses))
    held_3 = sum(from_3, packed_3[0])
    whole = b16(PANELS * B, PANELS * B)
    inverse = call(combine_kernel, (whole, whole), place, inverses, grams, limit=16)
    from_3 = [across(held_3, x) for x in range(1, chips)]
    from_3, inverse = lax.optimization_barrier((from_3, inverse))
    solved = b16(chips * mine, PANELS * B)
    dones = f32(chips, mine, width)
    kept = [kept_01[2 * h : 2 * h + 2] + kept_2[2 * h : 2 * h + 2] + kept_3[2 * h : 2 * h + 2] for h in range(2)]
    *solved, first = call(
        functools.partial(first_kernel, chips),
        (solved, solved, dones),
        place,
        *(*p_early, *inverse, held_3, *from_3, grid, *kept[0]),
        limit=24,
    )
    second = call(functools.partial(update_kernel, chips, 1), dones, place, grid, *solved, *kept[1], limit=20)
    result = jnp.zeros_like(eigvecs)
    for half, done in enumerate((first, second)):
        for x in range(chips):
            piece = across(done[x], x) if x else done[x]
            start = (chip ^ x) * 2 * width + (core ^ half) * width
            result = lax.dynamic_update_slice(result, piece, (0, start))
    return result


def solution(mesh):
    rows, cols = mesh.shape["row"], mesh.shape["col"]
    placed = (P(("row", "col"), None), P("col", "row"))

    def shards(eigvecs, reflectors):
        if cols == PANELS and reflectors.shape[0] == B and rows >= 4 and rows & (rows - 1) == 0 and B % (16 * rows) == 0:
            return panels_on_cols(eigvecs, reflectors, rows // 2)
        return general(eigvecs, reflectors)

    return jax.shard_map(shards, mesh=mesh, in_specs=placed, out_specs=P(("row", "col"), None), check_vma=False)
```
